256 devices in a mesh: seg: 8 (over y, x_lo), dp: 32 (over x_hi, z, core).
Axes of the slice: x: 4 (x_hi: 2, x_lo: 2; x = x_hi * 2 + x_lo), y: 4, z: 8, core: 2. Of those that a mesh axis runs over, the one named last changes fastest.
Arguments:
- segment_x: bfloat16 [32, 8, 256, 8192], P('dp', 'seg'), may hold values from -6 to 6
- header_x: bfloat16 [32, 256, 8192], P('dp', 'seg'), may hold values from -6 to 6
- queries: bfloat16 [32, 8, 256, 4096], P('dp', 'seg'), may hold values from -100 to 100
- keys: bfloat16 [32, 8, 256, 512], P('dp', 'seg'), may hold values from -6 to 6
- mem_queries: bfloat16 [32, 8, 128, 512], P('dp', 'seg'), may hold values from -100 to 100
- mem_keys: bfloat16 [32, 8, 128, 512], P('dp', 'seg'), may hold values from -6 to 6
- header_keys: bfloat16 [32, 256, 512], P('dp', 'seg'), may hold values from -6 to 6
- memory_init: float32 [32, 128, 512], P('dp'), may hold values from -6 to 6
- block_mask: int32 [32, 8, 2, 5], P('dp', 'seg'), may hold values from 0 to 1, as said below
- grad_out: bfloat16 [32, 8, 256, 4096], P('dp', 'seg'), may hold values from -6 to 6
- value_weight: bfloat16 [8192, 512], P('dp'), may hold values from -0.0625 to 0.0625
Outputs:
- attention: bfloat16 [32, 8, 256, 4096], P('dp', 'seg')
- value_grad: float32 [8192, 512], P('dp')
The draws below stay inside these ranges and needn't reach their ends.
Inputs may be any that keep to these rules, and one draw needn't show every extreme that they name: `block_mask`: the entry of a query block for the segment block on its diagonal is 1; entries for later segment blocks are 0.
All inputs are finite; a program needn't handle non-finite values.
Results may differ from the reference program's by a relative error of at most 0.0056.
Values may be sent and summed in bfloat16 or wider, within the bound.
A program may use at most 128 MiB of HBM per device.

```python
import jax
import jax.numpy as jnp
from jax import lax

D = 8192
HQ = 32
KVH = 4
HD = 128
MEM = 128
BLK = 128
SEG_LEN = 256
GROUP = 8
KVW = 512
HEADER = 256
BATCH = 32
SEGS = 8
NQB = 2
NHB = 2
NKB = 5


def keys_shared(key):
    shape = (BATCH, SEGS, SEG_LEN, KVH, HD)
    base = jnp.clip(jax.random.normal(jax.random.fold_in(key, 101), shape, jnp.float32), -6.0, 6.0)
    return base


def draw_keys(key, part):
    return keys_shared(key).reshape(BATCH, SEGS, SEG_LEN, KVH * HD).astype(jnp.bfloat16)


def draw_queries(key, part):
    shape = (BATCH, SEGS, SEG_LEN, KVH, GROUP, HD)
    base = jnp.clip(jax.random.normal(jax.random.fold_in(key, 102), shape, jnp.float32), -6.0, 6.0)
    return base.reshape(BATCH, SEGS, SEG_LEN, KVH * GROUP * HD).astype(jnp.bfloat16)


def draw_mem_queries(key, part):
    shape = (BATCH, SEGS, MEM, KVH, HD)
    base = jnp.clip(jax.random.normal(jax.random.fold_in(key, 104), shape, jnp.float32), -6.0, 6.0)
    return base.reshape(BATCH, SEGS, MEM, KVH * HD).astype(jnp.bfloat16)


def draw_block_mask(key, part):
    drawn = jax.random.randint(jax.random.fold_in(key, 106), (BATCH, SEGS, NQB, NKB), 0, 4)
    opened = (drawn > 0).astype(jnp.int32)
    query_block = jnp.arange(NQB)[:, None]
    seg_block = jnp.arange(NKB)[None, :] - NHB - 1
    diagonal = jnp.broadcast_to(seg_block == query_block, (BATCH, SEGS, NQB, NKB))
    future = jnp.broadcast_to(seg_block > query_block, (BATCH, SEGS, NQB, NKB))
    return jnp.where(diagonal, 1, jnp.where(future, 0, opened)).astype(jnp.int32)


def with_spikes(entries, own_key, source, target, shards_of, factor):
    def block_of(dim):
        return (jnp.arange(entries.shape[dim]) // (entries.shape[dim] // shards_of)).reshape((-1,) + (1,) * (entries.ndim - 1 - dim))

    first = jax.random.permutation(own_key, shards_of)[block_of(target)]
    far = (block_of(target) + shards_of // 2) % shards_of
    return jnp.where((block_of(source) == first) | (block_of(source) == far), factor * entries, entries)


def levels(stream_key, dims, cuts, least, high):
    def one(dim, blocks):
        draws = jax.random.uniform(jax.random.fold_in(jax.random.fold_in(stream_key, 6), dim), (blocks,), jnp.float32, least / len(cuts), high / len(cuts))
        return jnp.repeat(jnp.exp(draws), dims[dim] // blocks).reshape((-1,) + (1,) * (len(dims) - dim - 1))

    loudness = one(*cuts[0])
    for cut in cuts[1:]:
        loudness = loudness * one(*cut)
    return loudness


def normal_values(stream_key, dims, scale, limit, cuts=(), kind=jnp.bfloat16):
    level = levels(stream_key, dims, cuts, -0.22, 0.18) if cuts else 1.0
    array = jax.random.normal(stream_key, dims, jnp.float32) * scale * level
    return jnp.minimum(jnp.maximum(array, -limit), limit).astype(kind)


def gaussian_with(stream_key, shape, deviation, most, cuts, heavy, kind=jnp.bfloat16):
    array = deviation * jax.random.normal(stream_key, shape, jnp.float32)
    if cuts:
        array = array * levels(stream_key, shape, cuts, -0.22, 0.18)
    return jnp.clip(with_spikes(array, jax.random.fold_in(stream_key, 3), *heavy), -most, most).astype(kind)


def setup_inputs(seed: int = 0) -> dict:
    streams_of = jax.random.split(jax.random.key(seed), 12)
    segment_x = gaussian_with(streams_of[0], (BATCH, SEGS, SEG_LEN, D), 1.0, 6.0, ((0, 32), (1, 8)), (0, 3, 32, 2.75))
    header_x = gaussian_with(streams_of[1], (BATCH, HEADER, D), 1.0, 6.0, ((0, 32), (1, 8)), (0, 2, 32, 2.75))
    queries = draw_queries(jax.random.fold_in(streams_of[11], 71), 0)
    keys = draw_keys(jax.random.fold_in(streams_of[11], 71), 0)
    mem_queries = draw_mem_queries(jax.random.fold_in(streams_of[11], 71), 0)
    mem_keys = normal_values(streams_of[5], (BATCH, SEGS, MEM, KVW), 1.0, 6.0, ((0, 32), (1, 8)))
    header_keys = normal_values(streams_of[6], (BATCH, HEADER, KVW), 1.0, 6.0, ((0, 32), (1, 8)))
    memory_init = normal_values(streams_of[7], (BATCH, MEM, KVW), 1.0, 6.0, ((0, 32),), jnp.float32)
    block_mask = draw_block_mask(jax.random.fold_in(streams_of[11], 71), 0)
    grad_out = normal_values(streams_of[9], (BATCH, SEGS, SEG_LEN, HQ * HD), 1.0, 6.0, ((0, 32), (1, 8)))
    value_weight = normal_values(streams_of[10], (D, KVW), D ** -0.5, 0.0625, ((0, 32),))
    return {"segment_x": segment_x, "header_x": header_x, "queries": queries, "keys": keys, "mem_queries": mem_queries, "mem_keys": mem_keys, "header_keys": header_keys, "memory_init": memory_init, "block_mask": block_mask, "grad_out": grad_out, "value_weight": value_weight}


def masked_softmax(scores, allowed):
    kept_scores = jnp.where(allowed, scores, -1e30)
    largest = jnp.max(kept_scores, axis=-1, keepdims=True)
    weights = jnp.exp(kept_scores - largest) * allowed.astype(scores.dtype)
    return weights / jnp.sum(weights, axis=-1, keepdims=True)


def allowed_table(block_rows, seg_len, header_len, mem_len):
    header_blocks = header_len // BLK
    per_row = jnp.repeat(block_rows, BLK, axis=0)
    per_key = jnp.concatenate([
        jnp.repeat(per_row[:, :header_blocks], BLK, axis=1),
        jnp.repeat(per_row[:, header_blocks:header_blocks + 1], mem_len, axis=1),
        jnp.repeat(per_row[:, header_blocks + 1:], BLK, axis=1)], axis=1)
    position = jnp.arange(seg_len)
    causal = jnp.concatenate([
        jnp.ones((seg_len, header_len + mem_len), jnp.bool_),
        position[None, :] <= position[:, None]], axis=1)
    return (per_key > 0) & causal


def reference(segment_x, header_x, queries, keys, mem_queries, mem_keys, header_keys, memory_init, block_mask, grad_out, value_weight):
    kv_width = KVH * HD
    scale_factor = HD ** -0.5
    highest = lax.Precision.HIGHEST

    def one_sequence(running, items):
        seq_x, head_x, seq_q, seq_k, seq_mq, seq_mk, head_k, mem_init, seq_mask, seq_dout = items
        flat_x = seq_x.reshape(SEGS * SEG_LEN, D)
        values = jnp.dot(flat_x, value_weight, preferred_element_type=jnp.float32).astype(jnp.bfloat16).reshape(SEGS, SEG_LEN, KVH, HD)
        head_values = jnp.dot(head_x, value_weight, preferred_element_type=jnp.float32).astype(jnp.bfloat16).reshape(HEADER, KVH, HD)
        seg_keys = seq_k.reshape(SEGS, SEG_LEN, KVH, HD)
        read_scores = jnp.einsum("smgd,sjgd->sgmj", seq_mq.reshape(SEGS, MEM, KVH, HD).astype(jnp.float32), seg_keys.astype(jnp.float32), precision=highest) * scale_factor
        read_weights = lax.optimization_barrier(jax.nn.softmax(read_scores, axis=-1).astype(jnp.bfloat16)).astype(jnp.float32)
        readout = jnp.einsum("sgmj,sjgd->smgd", read_weights, values.astype(jnp.float32), precision=highest)
        running_sum = jnp.cumsum(readout, axis=0)
        earlier = jnp.concatenate([jnp.zeros_like(readout[:1]), running_sum[:-1]], axis=0)
        mem_values = (mem_init.reshape(1, MEM, KVH, HD) + earlier).astype(jnp.bfloat16)
        head_keys = head_k.reshape(HEADER, KVH, HD)

        def attend(pieces):
            seg_q, keys_here, values_here, mkeys, mvalues, mask_here, dout_here = pieces
            all_keys = jnp.concatenate([head_keys, mkeys.reshape(MEM, KVH, HD), keys_here], axis=0).astype(jnp.float32)
            all_values = jnp.concatenate([head_values, mvalues, values_here], axis=0).astype(jnp.float32)
            allowed = allowed_table(mask_here, SEG_LEN, HEADER, MEM)
            scores = jnp.einsum("igtd,jgd->gtij", seg_q.reshape(SEG_LEN, KVH, GROUP, HD).astype(jnp.float32), all_keys, precision=highest) * scale_factor
            weights = lax.optimization_barrier(masked_softmax(scores, allowed[None, None]).astype(jnp.bfloat16)).astype(jnp.float32)
            output = jnp.einsum("gtij,jgd->igtd", weights, all_values, precision=highest).reshape(SEG_LEN, HQ * HD).astype(jnp.bfloat16)
            key_grads = jnp.einsum("gtij,igtd->jgd", weights, dout_here.reshape(SEG_LEN, KVH, GROUP, HD).astype(jnp.float32), precision=highest)
            return output, key_grads

        outputs, key_grads = lax.map(attend, (seq_q, seg_keys, values, seq_mk, mem_values, seq_mask, seq_dout))
        head_grad = jnp.sum(key_grads[:, :HEADER], axis=0).reshape(HEADER, kv_width)
        mem_grad = key_grads[:, HEADER:HEADER + MEM]
        later_sum = jnp.cumsum(mem_grad[::-1], axis=0)[::-1]
        readout_grad = jnp.concatenate([later_sum[1:], jnp.zeros_like(mem_grad[:1])], axis=0)
        value_grads = key_grads[:, HEADER + MEM:] + jnp.einsum("sgmj,smgd->sjgd", read_weights, readout_grad, precision=highest)
        value_grads = value_grads.astype(jnp.bfloat16).reshape(SEGS * SEG_LEN, kv_width)
        weight_grad = jnp.dot(flat_x.T, value_grads, preferred_element_type=jnp.float32) + jnp.dot(head_x.T.astype(jnp.float32), head_grad, precision=highest, preferred_element_type=jnp.float32)
        return running + weight_grad, outputs

    value_grad, attention = lax.scan(one_sequence, jnp.zeros((D, kv_width), jnp.float32), (segment_x, header_x, queries, keys, mem_queries, mem_keys, header_keys, memory_init, block_mask, grad_out))
    return attention, value_grad
```

```python
import functools

import jax
import jax.numpy as jnp
from jax import lax
from jax.experimental import pallas as pl
from jax.experimental.pallas import tpu as pltpu
from jax.sharding import PartitionSpec as P

MESH = pl.DeviceIdType.MESH
BF = jnp.bfloat16
F32 = jnp.float32
NEG = -1e30
HD = 128
SEG = 256
MEM = 128
HDR = 256
G = 4
T = 8
NK = HDR + MEM + SEG
LOG2E = 1.4426950408889634
SCALE2 = HD ** (-0.5) * LOG2E


def device(x, y, z, c):
    return {"seg": y * 2 + x % 2, "dp": (x // 2) * 16 + z * 2 + c}


def kernel(
    seg_x,
    hdr_x,
    q_hbm,
    keys,
    memq,
    memk,
    hkeys,
    minit,
    mask,
    go_hbm,
    w_hbm,
    out_hbm,
    dw_ref,
    q_v,
    go_v,
    out_v,
    wts,
    kall,
    hk_all,
    bias,
    rw,
    kgt,
    xall,
    wb1,
    wb2,
    mg_send,
    mg_recv,
    hs_send,
    hs_recv,
    hg,
    hg_sib,
    vgt,
    vgcat,
    r1,
    r2,
    ra1,
    ra2,
    s1,
    s2,
    rb1,
    rb2,
    t1,
    t2,
    zr1,
    zr2,
    fall,
    acc,
    vrecv,
    v_all,
    hv_all,
    ro_send,
    ro_recv,
    vcat,
    load_sem,
    x_sem,
    seg_s,
    seg_r,
    mg_s,
    mg_r,
    hs_s,
    hs_r,
    sib_s,
    sib_r,
    z_s,
    z_r,
    ring_s,
    ring_r,
):
    s = lax.axis_index("seg")
    p = lax.axis_index("dp")
    y, xl = s // 2, s % 2
    xh, z, c = p // 16, (p // 2) % 8, p % 2
    x = xh * 2 + xl
    k_own = xh * 8 + z
    sib = {"seg": s, "dp": xh * 16 + z * 2 + (1 - c)}
    seg_peer = [{"seg": (s + j) % 8, "dp": p} for j in range(1, 8)]
    z_peer = [device(x, y, (z + j) % 8, c) for j in range(1, 8)]
    rings = {
        "x": (x, device((x + 1) % 4, y, z, c), device((x + 3) % 4, y, z, c)),
        "y": (y, device(x, (y + 1) % 4, z, c), device(x, (y + 3) % 4, z, c)),
    }
    sends = []

    def remote(src, dst, ssem, rsem, dev):
        return pltpu.make_async_remote_copy(
            src_ref=src,
            dst_ref=dst,
            send_sem=ssem,
            recv_sem=rsem,
            device_id=dev,
            device_id_type=MESH,
        )

    def go_out(src, dst, ssem, rsem, dev):
        copy = remote(src, dst, ssem, rsem, dev)
        copy.start()
        sends.append((None, copy))
        return copy

    loads = []
    for g in range(G):
        cols = pl.ds(g * 1024, 1024)
        a = pltpu.make_async_copy(q_hbm.at[0, 0, :, cols], q_v.at[:, cols], load_sem.at[2 * g])
        b = pltpu.make_async_copy(go_hbm.at[0, 0, :, cols], go_v.at[:, cols], load_sem.at[2 * g + 1])
        a.start()
        b.start()
        loads.append((a, b))

    @pl.loop(0, 16)
    def _(k):
        cols = pl.ds(pl.multiple_of((2 * k + c) * 256, 256), 256)
        pltpu.make_async_copy(
            seg_x.at[0, 0, :, cols], xall.at[k, pl.ds(0, 256)], load_sem.at[8]
        ).start()
        pltpu.make_async_copy(
            hdr_x.at[0, :, cols], xall.at[k, pl.ds(512, 32)], load_sem.at[9]
        ).start()

    w_row = s * 32
    own_w = [
        pltpu.make_async_copy(
            w_hbm.at[pl.ds(pl.multiple_of(w_row + 16 * h, 16), 16)], dst, load_sem.at[10 + h]
        )
        for h, dst in ((0, wb1.at[y, x, z]), (1, wb2.at[x, y, z]))
    ]
    for copy in own_w:
        copy.start()

    barrier = pltpu.get_barrier_semaphore()
    greeted = [sib, rings["x"][1], rings["x"][2]] + seg_peer + z_peer
    for dev in greeted:
        pl.semaphore_signal(barrier, inc=1, device_id=dev, device_id_type=MESH)
    pl.semaphore_wait(barrier, len(greeted))

    hk_copies = [
        go_out(hkeys.at[0], hk_all.at[s], seg_s.at[0, j], seg_r.at[0, j], seg_peer[j])
        for j in range(7)
    ]
    wz_copies = []
    for j in range(7):
        for h, dst in ((0, wb1.at[y, x, z]), (1, wb2.at[x, y, z])):
            src = w_hbm.at[pl.ds(pl.multiple_of(w_row + 16 * h, 16), 16)]
            wz_copies.append(go_out(src, dst, z_s.at[h, j], z_r.at[h, j], z_peer[j]))

    @pl.loop(0, 16)
    def _(k):
        cols = pl.ds(pl.multiple_of((2 * k + 1 - c) * 256, 256), 256)
        remote(
            seg_x.at[0, 0, :, cols], xall.at[k, pl.ds(256, 256)], x_sem.at[0], x_sem.at[1], sib
        ).start()
        remote(
            hdr_x.at[0, :, cols], xall.at[k, pl.ds(544, 32)], x_sem.at[2], x_sem.at[3], sib
        ).start()

    hk_all[s] = hkeys[0]
    for k in range(16):
        xall[k, 576:640] = jnp.zeros((64, 256), BF)

    rows_i = lax.broadcasted_iota(jnp.int32, (128, 128), 0)
    cols_i = lax.broadcasted_iota(jnp.int32, (128, 128), 1)
    causal = jnp.where(cols_i <= rows_i, 0.0, NEG).astype(F32)
    for qb in range(2):
        for kb in range(5):
            level = jnp.where(mask[0, 0, qb, kb] > 0, 0.0, NEG).astype(F32)
            block = jnp.full((128, 128), level, F32)
            if kb == 3 + qb:
                block = jnp.minimum(block, causal)
            bias[qb * 128 : qb * 128 + 128, kb * 128 : kb * 128 + 128] = block

    def softmax2(scores):
        top = jnp.max(scores, axis=-1, keepdims=True)
        e = jnp.exp2(scores - top)
        return e * (1.0 / jnp.sum(e, axis=-1, keepdims=True))

    nt = (((1,), (1,)), ((), ()))
    tn = (((0,), (0,)), ((), ()))
    for g in range(G):
        cg = slice(g * 128, g * 128 + 128)
        kall[g, 256:384] = memk[0, 0, :, cg]
        kall[g, 384:640] = keys[0, 0, :, cg]
        sc = lax.dot_general(memq[0, 0, :, cg], keys[0, 0, :, cg], nt, preferred_element_type=F32)
        rw[g] = softmax2(sc * SCALE2).astype(BF)

    for copy in hk_copies:
        copy.wait_recv()
    for g in range(G):
        for t in range(8):
            kall[g, t * 32 : t * 32 + 32] = hk_all[t, :, g * 128 : g * 128 + 128]

    def ag_start(buf, axis, n, st):
        r, right, left = rings[axis]
        lo, hi = pl.ds(0, n // 2), pl.ds(n // 2, n // 2)
        S, R = ring_s.at[st], ring_r.at[st]
        cp = {}
        cp["Llo"] = go_out(buf.at[r, lo], buf.at[r, lo], S.at[0], R.at[0], right)
        cp["Rhi"] = go_out(buf.at[r, hi], buf.at[r, hi], S.at[3], R.at[3], left)
        cp["Lhi"] = go_out(buf.at[r, hi], buf.at[r, hi], S.at[1], R.at[1], right)
        cp["Rlo"] = go_out(buf.at[r, lo], buf.at[r, lo], S.at[2], R.at[2], left)
        return cp

    def ag_forward(buf, axis, n, st, cp):
        r, right, left = rings[axis]
        lo, hi = pl.ds(0, n // 2), pl.ds(n // 2, n // 2)
        S, R = ring_s.at[st], ring_r.at[st]
        before, after = (r + 3) % 4, (r + 1) % 4
        cp["Llo"].wait_recv()
        cp["FL"] = go_out(buf.at[before, lo], buf.at[before, lo], S.at[4], R.at[4], right)
        cp["Rhi"].wait_recv()
        cp["FR"] = go_out(buf.at[after, hi], buf.at[after, hi], S.at[5], R.at[5], left)

    def ag_end(cp):
        for name in ("Lhi", "Rlo", "FL", "FR"):
            cp[name].wait_recv()

    def rs_start(buf, land, axis, n, st):
        r, right, left = rings[axis]
        lo, hi = pl.ds(0, n // 2), pl.ds(n // 2, n // 2)
        S, R = ring_s.at[st], ring_r.at[st]
        far, after, before = (r + 2) % 4, (r + 1) % 4, (r + 3) % 4
        cp = {}
        cp["PL"] = go_out(buf.at[far, lo], land.at[0], S.at[0], R.at[0], right)
        cp["PR"] = go_out(buf.at[far, hi], land.at[1], S.at[1], R.at[1], left)
        cp["Lhi"] = go_out(buf.at[after, hi], land.at[3], S.at[3], R.at[3], right)
        cp["Rlo"] = go_out(buf.at[before, lo], land.at[4], S.at[4], R.at[4], left)
        return cp

    def rs_forward(buf, land, axis, n, st, cp):
        r, right, left = rings[axis]
        half = n // 2
        lo, hi = pl.ds(0, half), pl.ds(half, half)
        S, R = ring_s.at[st], ring_r.at[st]
        after, before = (r + 1) % 4, (r + 3) % 4
        cp["PL"].wait_recv()

        @pl.loop(0, half)
        def _(i):
            a = buf[after, i].astype(F32) + land[0, i].astype(F32)
            buf[after, i] = a.astype(BF)

        cp["Llo"] = go_out(buf.at[after, lo], land.at[2], S.at[2], R.at[2], right)
        cp["PR"].wait_recv()

        @pl.loop(0, half)
        def _(i):
            a = buf[before, half + i].astype(F32) + land[1, i].astype(F32)
            buf[before, half + i] = a.astype(BF)

        cp["Rhi"] = go_out(buf.at[before, hi], land.at[5], S.at[5], R.at[5], left)

    def rs_end(buf, land, out, axis, n, cp):
        r = rings[axis][0]
        half = n // 2
        for name in ("Lhi", "Rlo", "Llo", "Rhi"):
            cp[name].wait_recv()
        for part in range(2):

            @pl.loop(0, half)
            def _(i):
                a = buf[r, half * part + i].astype(F32)
                a = a + land[2 + part, i].astype(F32) + land[4 + part, i].astype(F32)
                out[half * part + i] = a.astype(BF)

    mg_copies = {}
    hs_copies = {}

    def attend(g):
        loads[g][0].wait()
        loads[g][1].wait()
        kgt[g] = jnp.zeros((128, NK), F32)

        @pl.loop(0, T)
        def _(t):
            h = g * T + t
            cols = pl.ds(pl.multiple_of(h * 128, 128), 128)
            for qb in range(2):
                nk = 512 + 128 * qb
                rows = slice(qb * 128, qb * 128 + 128)
                sc = lax.dot_general(
                    q_v[rows, cols], kall[g, 0:nk], nt, preferred_element_type=F32
                )
                wt = softmax2(sc * SCALE2 + bias[rows, 0:nk]).astype(BF)
                wts[h, rows, 0:nk] = wt
                if qb == 0:
                    wts[h, rows, 512:640] = jnp.zeros((128, 128), BF)
            kgt[g] += lax.dot_general(go_v[:, cols], wts[h], tn, preferred_element_type=F32)

        mg_send[g] = kgt[g, :, HDR : HDR + MEM].astype(BF)
        for j in range(7):
            copy = remote(
                mg_send.at[g], mg_recv.at[s, g], mg_s.at[g, j], mg_r.at[g, j], seg_peer[j]
            )
            earlier = (s + j + 1) % 8 < s
            pl.when(earlier)(copy.start)
            sends.append((earlier, copy))
            mg_copies[g, j] = copy
        hs_send[g] = kgt[g, :, 0:HDR].T.astype(BF).reshape(8, 32, 128)
        for j in range(7):
            peer = (s + j + 1) % 8
            hs_copies[g, j] = go_out(
                hs_send.at[g, peer], hs_recv.at[g, j], hs_s.at[g, j], hs_r.at[g, j], seg_peer[j]
            )

    sib_copies = []

    def close_group(g):
        rog = acc.at[0:128, 0:128]
        rog[...] = jnp.zeros((128, 128), F32)
        for j in range(7):
            origin = (s + 7 - j) % 8

            @pl.when(origin > s)
            def _():
                mg_copies[g, j].wait_recv()
                rog[...] += mg_recv[origin, g].astype(F32)

        back = jnp.dot(rog[...].astype(BF), rw[g], preferred_element_type=F32)
        vgt[0, g] = (kgt[g, :, HDR + MEM : NK] + back).astype(BF)
        sib_copies.append(go_out(vgt.at[0, g], vgt.at[1, g], sib_s.at[g], sib_r.at[g], sib))
        total = hs_send[g, s].astype(F32)
        for j in range(7):
            hs_copies[g, j].wait_recv()
            total = total + hs_recv[g, j].astype(F32)
        hg[g] = total.astype(BF)
        sib_copies.append(go_out(hg.at[g], hg_sib.at[g], sib_s.at[4 + g], sib_r.at[4 + g], sib))

    attend(0)
    for copy in own_w:
        copy.wait()
    for copy in wz_copies:
        copy.wait_recv()
    wx1 = ag_start(wb1.at[y], "x", 8, 0)
    wy2 = ag_start(wb2.at[x], "y", 8, 1)
    attend(1)
    ag_forward(wb1.at[y], "x", 8, 0, wx1)
    ag_forward(wb2.at[x], "y", 8, 1, wy2)
    close_group(0)
    attend(2)
    ag_end(wx1)
    ag_end(wy2)
    wy1 = ag_start(wb1, "y", 4, 2)
    wx2 = ag_start(wb2, "x", 4, 3)
    close_group(1)
    attend(3)
    close_group(2)
    ag_forward(wb1, "y", 4, 2, wy1)
    ag_forward(wb2, "x", 4, 3, wx2)
    close_group(3)

    pltpu.make_async_copy(
        xall.at[:, pl.ds(0, 256)], xall.at[:, pl.ds(0, 256)], load_sem.at[8]
    ).wait()
    pltpu.make_async_copy(
        xall.at[:, pl.ds(512, 32)], xall.at[:, pl.ds(512, 32)], load_sem.at[9]
    ).wait()
    sib_x = remote(
        xall.at[:, pl.ds(0, 256)], xall.at[:, pl.ds(256, 256)], x_sem.at[0], x_sem.at[1], sib
    )
    sib_hx = remote(
        xall.at[:, pl.ds(512, 32)], xall.at[:, pl.ds(544, 32)], x_sem.at[2], x_sem.at[3], sib
    )
    sib_x.wait_recv()
    sib_hx.wait_recv()
    for copy in sib_copies:
        copy.wait_recv()
    for g in range(G):
        rg = slice(g * 128, g * 128 + 128)
        vgcat[rg, 0:256] = vgt[0, g]
        vgcat[rg, 256:512] = vgt[1, g]
        head = jnp.concatenate(
            [hg[g].astype(F32), hg_sib[g].astype(F32), jnp.zeros((64, 128), F32)], axis=0
        )
        vgcat[rg, 512:640] = head.T.astype(BF)

    @pl.loop(0, 16)
    def _(k):
        kh, kz = k // 8, k % 8
        grad = jnp.dot(vgcat[...], xall[k], preferred_element_type=F32).astype(BF)
        for yy in range(4):
            for xx in range(2):
                i = yy * 2 + xx
                rows = jnp.concatenate(
                    [grad[g * 128 + i * 16 : g * 128 + i * 16 + 16] for g in range(G)], axis=0
                )
                r1[yy, kh * 2 + xx, kz] = rows[:, 0:128]
                r2[kh * 2 + xx, yy, kz] = rows[:, 128:256]

    gy1 = rs_start(r1, ra1, "y", 4, 4)
    gx2 = rs_start(r2, ra2, "x", 4, 5)

    ag_end(wy1)
    ag_end(wx2)
    for q in range(4):
        xs, ws = [], []
        for k in range(4 * q, 4 * q + 4):
            kh, kz = k // 8, k % 8
            xs.append(xall[k, 0:576])
            for yy in range(4):
                for xx in range(2):
                    ws.append(wb1[yy, kh * 2 + xx, kz])
                    ws.append(wb2[kh * 2 + xx, yy, kz])
        part = jnp.dot(
            jnp.concatenate(xs, axis=1), jnp.concatenate(ws, axis=0), preferred_element_type=F32
        )
        if q == 0:
            acc[...] = part
        else:
            acc[...] += part
    va = go_out(
        acc.at[pl.ds(256, 256)], vrecv.at[pl.ds(0, 256)], sib_s.at[8], sib_r.at[8], sib
    )
    vb = go_out(acc.at[pl.ds(544, 32)], vrecv.at[pl.ds(256, 32)], sib_s.at[9], sib_r.at[9], sib)
    va.wait_recv()
    vb.wait_recv()
    hv_all[s] = (acc[512:544] + vrecv[256:288]).astype(BF)
    hv_copies = [
        go_out(hv_all.at[s], hv_all.at[s], seg_s.at[1, j], seg_r.at[1, j], seg_peer[j])
        for j in range(7)
    ]
    v_all[...] = (acc[0:256] + vrecv[0:256]).astype(BF)
    for g in range(G):
        cg = slice(g * 128, g * 128 + 128)
        ro_send[:, cg] = jnp.dot(rw[g], v_all[:, cg], preferred_element_type=F32).astype(BF)
    ro_copies = []
    for j in range(7):
        copy = remote(ro_send, ro_recv.at[s], seg_s.at[2, j], seg_r.at[2, j], seg_peer[j])
        after = (s + j + 1) % 8 > s
        pl.when(after)(copy.start)
        sends.append((after, copy))
        ro_copies.append(copy)

    rs_forward(r1, ra1, "y", 4, 4, gy1)
    rs_forward(r2, ra2, "x", 4, 5, gx2)

    mem = minit[0]
    memory = acc.at[0:128, :]
    for copy in sends:
        if copy[1] is va:
            copy[1].wait_send()
    memory[...] = mem
    for j in range(7):
        origin = (s + 7 - j) % 8

        @pl.when(origin < s)
        def _():
            ro_copies[j].wait_recv()
            memory[...] += ro_recv[origin].astype(F32)

    for copy in hv_copies:
        copy.wait_recv()
    for g in range(G):
        cg = slice(g * 128, g * 128 + 128)
        for t in range(8):
            vcat[g, t * 32 : t * 32 + 32] = hv_all[t, :, cg]
        vcat[g, 256:384] = memory[:, cg].astype(BF)
        vcat[g, 384:640] = v_all[:, cg]

    out_copies = []

    def finish(g):
        @pl.loop(0, T)
        def _(t):
            h = g * T + t
            cols = pl.ds(pl.multiple_of(h * 128, 128), 128)
            out_v[:, cols] = jnp.dot(wts[h], vcat[g], preferred_element_type=F32).astype(BF)

        cols = pl.ds(g * 1024, 1024)
        copy = pltpu.make_async_copy(
            out_v.at[:, cols], out_hbm.at[0, 0, :, cols], load_sem.at[12 + g]
        )
        copy.start()
        out_copies.append(copy)

    finish(0)
    finish(1)
    rs_end(r1, ra1, s1, "y", 4, gy1)
    gx1 = rs_start(s1, rb1, "x", 8, 6)
    rs_end(r2, ra2, s2, "x", 4, gx2)
    gy2 = rs_start(s2, rb2, "y", 8, 7)
    finish(2)
    rs_forward(s1, rb1, "x", 8, 6, gx1)
    rs_forward(s2, rb2, "y", 8, 7, gy2)
    finish(3)
    rs_end(s1, rb1, t1, "x", 8, gx1)
    gz = []
    for j in range(7):
        to = (z + j + 1) % 8
        gz.append(go_out(t1.at[to], zr1.at[j], z_s.at[2, j], z_r.at[2, j], z_peer[j]))
    rs_end(s2, rb2, t2, "y", 8, gy2)
    for j in range(7):
        to = (z + j + 1) % 8
        gz.append(go_out(t2.at[to], zr2.at[j], z_s.at[3, j], z_r.at[3, j], z_peer[j]))
    for copy in gz:
        copy.wait_recv()
    for t_ref, zr, cols in ((t1, zr1, slice(0, 128)), (t2, zr2, slice(128, 256))):
        total = t_ref[z].astype(F32)
        for j in range(7):
            total = total + zr[j].astype(F32)
        fall[s, :, cols] = total
    f_copies = [
        go_out(fall.at[s], fall.at[s], seg_s.at[3, j], seg_r.at[3, j], seg_peer[j])
        for j in range(7)
    ]
    for copy in f_copies:
        copy.wait_recv()
    for g in range(G):
        rows = jnp.concatenate([fall[i, g * 16 : g * 16 + 16] for i in range(8)], axis=0)
        dw_ref[:, g * 128 : g * 128 + 128] = rows.T

    for copy in out_copies:
        copy.wait()
    sib_x.wait_send()
    sib_hx.wait_send()
    for condition, copy in sends:
        if copy is va:
            continue
        if condition is None:
            copy.wait_send()
        else:
            pl.when(condition)(copy.wait_send)


def per_device(*args):
    vmem = pl.BlockSpec(memory_space=pltpu.VMEM)
    hbm = pl.BlockSpec(memory_space=pl.ANY)
    smem = pl.BlockSpec(memory_space=pltpu.SMEM)
    V = pltpu.VMEM
    dma = pltpu.SemaphoreType.DMA
    return pl.pallas_call(
        kernel,
        out_shape=(
            jax.ShapeDtypeStruct((1, 1, SEG, 4096), BF),
            jax.ShapeDtypeStruct((256, 512), F32),
        ),
        in_specs=[hbm, hbm, hbm, vmem, vmem, vmem, vmem, vmem, smem, hbm, hbm],
        out_specs=(hbm, vmem),
        scratch_shapes=[
            V((SEG, 4096), BF),
            V((SEG, 4096), BF),
            V((SEG, 4096), BF),
            V((32, SEG, NK), BF),
            V((G, NK, HD), BF),
            V((8, 32, 512), BF),
            V((SEG, NK), F32),
            V((G, MEM, SEG), BF),
            V((G, HD, NK), F32),
            V((16, 640, 256), BF),
            V((4, 4, 8, 16, 512), BF),
            V((4, 4, 8, 16, 512), BF),
            V((G, HD, MEM), BF),
            V((8, G, HD, MEM), BF),
            V((G, 8, 32, HD), BF),
            V((G, 7, 32, HD), BF),
            V((G, 32, HD), BF),
            V((G, 32, HD), BF),
            V((2, G, HD, SEG), BF),
            V((512, 640), BF),
            V((4, 4, 8, 64, 128), BF),
            V((4, 4, 8, 64, 128), BF),
            V((6, 2, 8, 64, 128), BF),
            V((6, 2, 8, 64, 128), BF),
            V((4, 8, 64, 128), BF),
            V((4, 8, 64, 128), BF),
            V((6, 4, 64, 128), BF),
            V((6, 4, 64, 128), BF),
            V((8, 64, 128), BF),
            V((8, 64, 128), BF),
            V((7, 64, 128), BF),
            V((7, 64, 128), BF),
            V((8, 64, 256), F32),
            V((576, 512), F32),
            V((288, 512), F32),
            V((SEG, 512), BF),
            V((8, 32, 512), BF),
            V((MEM, 512), BF),
            V((8, MEM, 512), BF),
            V((G, NK, HD), BF),
            dma((16,)),
            dma((4,)),
            dma((4, 7)),
            dma((4, 7)),
            dma((G, 7)),
            dma((G, 7)),
            dma((G, 7)),
            dma((G, 7)),
            dma((10,)),
            dma((10,)),
            dma((4, 7)),
            dma((4, 7)),
            dma((8, 6)),
            dma((8, 6)),
        ],
        compiler_params=pltpu.CompilerParams(
            collective_id=0, has_side_effects=True, vmem_limit_bytes=56 * 1024 * 1024
        ),
    )(*args)


def solution(mesh):
    placed = (
        P("dp", "seg", None, None),
        P("dp", "seg", None),
        P("dp", "seg", None, None),
        P("dp", "seg", None, None),
        P("dp", "seg", None, None),
        P("dp", "seg", None, None),
        P("dp", "seg", None),
        P("dp", None, None),
        P("dp", "seg", None, None),
        P("dp", "seg", None, None),
        P("dp", None),
    )
    return jax.shard_map(
        per_device,
        mesh=mesh,
        in_specs=placed,
        out_specs=(P("dp", "seg", None, None), P("dp", None)),
        check_vma=False,
    )
```

```python
import functools

import jax
import jax.numpy as jnp
from jax import lax
from jax.experimental import pallas as pl
from jax.experimental.pallas import tpu as pltpu
from jax.sharding import PartitionSpec as P

MESH = pl.DeviceIdType.MESH
BF = jnp.bfloat16
F32 = jnp.float32
NEG = -1e30
HD = 128
SEG = 256
MEM = 128
HDR = 256
G = 4
T = 8
HEADS = 4
NK = HDR + MEM + SEG
LOG2E = 1.4426950408889634
SCALE2 = HD ** (-0.5) * LOG2E


def device(x, y, z, c):
    return {"seg": y * 2 + x % 2, "dp": (x // 2) * 16 + z * 2 + c}


def kernel(
    seg_x,
    hdr_x,
    q_hbm,
    keys,
    memq,
    memk,
    hkeys,
    minit,
    mask,
    go_hbm,
    w_hbm,
    out_hbm,
    dw_ref,
    q_v,
    go_v,
    out_v,
    wts,
    kall,
    hk_all,
    bias,
    rw,
    kgt,
    xall,
    wb1,
    wb2,
    mg_send,
    mg_recv,
    pm_send,
    pm_recv,
    rog,
    hs_send,
    hs_recv,
    hg,
    hg_sib,
    vgt,
    vgcat,
    r1,
    r2,
    ra1,
    ra2,
    da1,
    da2,
    s1,
    s2,
    rb1,
    rb2,
    t1,
    t2,
    zr1,
    zr2,
    fall,
    acc,
    vrecv,
    v_all,
    hv_all,
    ro_send,
    ro_recv,
    po_send,
    po_recv,
    memory,
    vcat,
    load_sem,
    x_sem,
    seg_s,
    seg_r,
    f_s,
    f_r,
    mg_s,
    mg_r,
    hs_s,
    hs_r,
    sib_s,
    sib_r,
    z_s,
    z_r,
    ring_s,
    ring_r,
):
    s = lax.axis_index("seg")
    p = lax.axis_index("dp")
    y, xl = s // 2, s % 2
    xh, z, c = p // 16, (p // 2) % 8, p % 2
    x = xh * 2 + xl
    k_own = xh * 8 + z
    sib = {"seg": s, "dp": xh * 16 + z * 2 + (1 - c)}
    seg_peer = [{"seg": (s + j) % 8, "dp": p} for j in range(1, 8)]
    pair = {"seg": y * 2 + (1 - xl), "dp": p}
    below = [{"seg": ((y + 4 - j) % 4) * 2 + xl, "dp": p} for j in (1, 2, 3)]
    above = [{"seg": ((y + j) % 4) * 2 + xl, "dp": p} for j in (1, 2, 3)]
    z_peer = [device(x, y, (z + j) % 8, c) for j in range(1, 8)]
    rings = {
        "x": (x, device((x + 1) % 4, y, z, c), device((x + 3) % 4, y, z, c)),
        "y": (y, device(x, (y + 1) % 4, z, c), device(x, (y + 3) % 4, z, c)),
    }
    sends = []

    def remote(src, dst, ssem, rsem, dev):
        return pltpu.make_async_remote_copy(
            src_ref=src,
            dst_ref=dst,
            send_sem=ssem,
            recv_sem=rsem,
            device_id=dev,
            device_id_type=MESH,
        )

    def go_out(src, dst, ssem, rsem, dev):
        copy = remote(src, dst, ssem, rsem, dev)
        copy.start()
        sends.append((None, copy))
        return copy

    loads = []
    for g in range(G):
        cols = pl.ds(g * 1024, 1024)
        a = pltpu.make_async_copy(q_hbm.at[0, 0, :, cols], q_v.at[:, cols], load_sem.at[2 * g])
        b = pltpu.make_async_copy(go_hbm.at[0, 0, :, cols], go_v.at[:, cols], load_sem.at[2 * g + 1])
        a.start()
        b.start()
        loads.append((a, b))

    @pl.loop(0, 16)
    def _(k):
        cols = pl.ds(pl.multiple_of((2 * k + c) * 256, 256), 256)
        pltpu.make_async_copy(
            seg_x.at[0, 0, :, cols], xall.at[k, pl.ds(0, 256)], load_sem.at[8]
        ).start()
        pltpu.make_async_copy(
            hdr_x.at[0, :, cols], xall.at[k, pl.ds(512, 32)], load_sem.at[9]
        ).start()

    w_row = s * 32
    own_w = [
        pltpu.make_async_copy(
            w_hbm.at[pl.ds(pl.multiple_of(w_row + 16 * h, 16), 16)], dst, load_sem.at[10 + h]
        )
        for h, dst in ((0, wb1.at[y, x, z]), (1, wb2.at[x, y, z]))
    ]
    for copy in own_w:
        copy.start()

    barrier = pltpu.get_barrier_semaphore()
    across = [device((x + j) % 4, y, z, c) for j in (1, 2, 3)]
    greeted = [sib] + across + seg_peer + z_peer
    for dev in greeted:
        pl.semaphore_signal(barrier, inc=1, device_id=dev, device_id_type=MESH)
    pl.semaphore_wait(barrier, len(greeted))

    hk_copies = [
        go_out(hkeys.at[0], hk_all.at[s], seg_s.at[0, j], seg_r.at[0, j], seg_peer[j])
        for j in range(7)
    ]
    wz_copies = []
    for j in range(7):
        for h, dst in ((0, wb1.at[y, x, z]), (1, wb2.at[x, y, z])):
            src = w_hbm.at[pl.ds(pl.multiple_of(w_row + 16 * h, 16), 16)]
            wz_copies.append(go_out(src, dst, z_s.at[h, j], z_r.at[h, j], z_peer[j]))

    @pl.loop(0, 16)
    def _(k):
        cols = pl.ds(pl.multiple_of((2 * k + 1 - c) * 256, 256), 256)
        remote(
            seg_x.at[0, 0, :, cols], xall.at[k, pl.ds(256, 256)], x_sem.at[0], x_sem.at[1], sib
        ).start()
        remote(
            hdr_x.at[0, :, cols], xall.at[k, pl.ds(544, 32)], x_sem.at[2], x_sem.at[3], sib
        ).start()

    hk_all[s] = hkeys[0]
    for k in range(16):
        xall[k, 576:640] = jnp.zeros((64, 256), BF)

    rows_i = lax.broadcasted_iota(jnp.int32, (128, 128), 0)
    cols_i = lax.broadcasted_iota(jnp.int32, (128, 128), 1)
    causal = jnp.where(cols_i <= rows_i, 0.0, NEG).astype(F32)
    for qb in range(2):
        for kb in range(5):
            level = jnp.where(mask[0, 0, qb, kb] > 0, 0.0, NEG).astype(F32)
            block = jnp.full((128, 128), level, F32)
            if kb == 3 + qb:
                block = jnp.minimum(block, causal)
            bias[qb * 128 : qb * 128 + 128, kb * 128 : kb * 128 + 128] = block

    def softmax2(scores):
        top = jnp.max(scores, axis=-1, keepdims=True)
        e = jnp.exp2(scores - top)
        return e * (1.0 / jnp.sum(e, axis=-1, keepdims=True))

    nt = (((1,), (1,)), ((), ()))
    tn = (((0,), (0,)), ((), ()))
    for g in range(G):
        cg = slice(g * 128, g * 128 + 128)
        kall[g, 256:384] = memk[0, 0, :, cg]
        kall[g, 384:640] = keys[0, 0, :, cg]
        sc = lax.dot_general(memq[0, 0, :, cg], keys[0, 0, :, cg], nt, preferred_element_type=F32)
        rw[g] = softmax2(sc * SCALE2).astype(BF)

    for copy in hk_copies:
        copy.wait_recv()
    for g in range(G):
        for t in range(8):
            kall[g, t * 32 : t * 32 + 32] = hk_all[t, :, g * 128 : g * 128 + 128]

    def ag_start(buf, axis, n, st):
        r, right, left = rings[axis]
        lo, hi = pl.ds(0, n // 2), pl.ds(n // 2, n // 2)
        S, R = ring_s.at[st], ring_r.at[st]
        cp = {}
        cp["Llo"] = go_out(buf.at[r, lo], buf.at[r, lo], S.at[0], R.at[0], right)
        cp["Rhi"] = go_out(buf.at[r, hi], buf.at[r, hi], S.at[3], R.at[3], left)
        cp["Lhi"] = go_out(buf.at[r, hi], buf.at[r, hi], S.at[1], R.at[1], right)
        cp["Rlo"] = go_out(buf.at[r, lo], buf.at[r, lo], S.at[2], R.at[2], left)
        return cp

    def ag_forward(buf, axis, n, st, cp):
        r, right, left = rings[axis]
        lo, hi = pl.ds(0, n // 2), pl.ds(n // 2, n // 2)
        S, R = ring_s.at[st], ring_r.at[st]
        before, after = (r + 3) % 4, (r + 1) % 4
        cp["Llo"].wait_recv()
        cp["FL"] = go_out(buf.at[before, lo], buf.at[before, lo], S.at[4], R.at[4], right)
        cp["Rhi"].wait_recv()
        cp["FR"] = go_out(buf.at[after, hi], buf.at[after, hi], S.at[5], R.at[5], left)

    def ag_end(cp):
        for name in ("Lhi", "Rlo", "FL", "FR"):
            cp[name].wait_recv()

    around = {
        "x": (x, [device((x + j) % 4, y, z, c) for j in (1, 2, 3)]),
        "y": (y, [device(x, (y + j) % 4, z, c) for j in (1, 2, 3)]),
    }

    def ag_direct(buf, axis, st):
        r, to = around[axis]
        S, R = ring_s.at[st], ring_r.at[st]
        return [go_out(buf.at[r], buf.at[r], S.at[j], R.at[j], to[j]) for j in (1, 0, 2)]

    def rs_direct(buf, land, axis, st):
        r, to = around[axis]
        S, R = ring_s.at[st], ring_r.at[st]
        return [
            go_out(buf.at[(r + j + 1) % 4], land.at[j], S.at[j], R.at[j], to[j])
            for j in (1, 0, 2)
        ]

    def rs_sum(buf, land, out, axis, copies):
        for copy in copies:
            copy.wait_recv()
        total = buf[around[axis][0]].astype(F32)
        for j in range(3):
            total = total + land[j].astype(F32)
        out[...] = total.astype(BF)

    def rs_start(buf, land, axis, n, st):
        r, right, left = rings[axis]
        lo, hi = pl.ds(0, n // 2), pl.ds(n // 2, n // 2)
        S, R = ring_s.at[st], ring_r.at[st]
        far, after, before = (r + 2) % 4, (r + 1) % 4, (r + 3) % 4
        cp = {}
        cp["PL"] = go_out(buf.at[far, lo], land.at[0], S.at[0], R.at[0], right)
        cp["PR"] = go_out(buf.at[far, hi], land.at[1], S.at[1], R.at[1], left)
        cp["Lhi"] = go_out(buf.at[after, hi], land.at[3], S.at[3], R.at[3], right)
        cp["Rlo"] = go_out(buf.at[before, lo], land.at[4], S.at[4], R.at[4], left)
        return cp

    def rs_forward(buf, land, axis, n, st, cp):
        r, right, left = rings[axis]
        half = n // 2
        lo, hi = pl.ds(0, half), pl.ds(half, half)
        S, R = ring_s.at[st], ring_r.at[st]
        after, before = (r + 1) % 4, (r + 3) % 4
        cp["PL"].wait_recv()
        buf[after, lo] = (buf[after, lo].astype(F32) + land[0].astype(F32)).astype(BF)
        cp["Llo"] = go_out(buf.at[after, lo], land.at[2], S.at[2], R.at[2], right)
        cp["PR"].wait_recv()
        buf[before, hi] = (buf[before, hi].astype(F32) + land[1].astype(F32)).astype(BF)
        cp["Rhi"] = go_out(buf.at[before, hi], land.at[5], S.at[5], R.at[5], left)

    def rs_end(buf, land, out, axis, n, cp):
        r = rings[axis][0]
        half = n // 2
        for name in ("Lhi", "Rlo", "Llo", "Rhi"):
            cp[name].wait_recv()
        for part in range(2):
            here = pl.ds(half * part, half)
            a = buf[r, here].astype(F32) + land[2 + part].astype(F32)
            out[here] = (a + land[4 + part].astype(F32)).astype(BF)

    def guarded(condition, src, dst, ssem, rsem, dev):
        copy = remote(src, dst, ssem, rsem, dev)
        pl.when(condition)(copy.start)
        sends.append((condition, copy))
        return copy

    mg_copies = {}
    pm_copies = {}
    hs_copies = {}
    sib_copies = {}

    def attend(g, part):
        if part == 0:
            loads[g][0].wait()
            loads[g][1].wait()
            kgt[g] = jnp.zeros((128, NK), F32)

        @pl.loop(0, T // 2 // HEADS)
        def _(t):
            for u in range(HEADS):
                h = g * T + part * (T // 2) + t * HEADS + u
                cols = pl.ds(pl.multiple_of(h * 128, 128), 128)
                for qb in range(2):
                    nk = 512 + 128 * qb
                    rows = slice(qb * 128, qb * 128 + 128)
                    sc = lax.dot_general(
                        q_v[rows, cols], kall[g, 0:nk], nt, preferred_element_type=F32
                    )
                    wt = softmax2(sc * SCALE2 + bias[rows, 0:nk]).astype(BF)
                    wts[h, rows, 0:nk] = wt
                    if qb == 0:
                        wts[h, rows, 512:640] = jnp.zeros((128, 128), BF)
            for u in range(HEADS):
                h = g * T + part * (T // 2) + t * HEADS + u
                cols = pl.ds(pl.multiple_of(h * 128, 128), 128)
                kgt[g] += lax.dot_general(go_v[:, cols], wts[h], tn, preferred_element_type=F32)

        if part == 0:
            return
        mg_send[g] = kgt[g, :, HDR : HDR + MEM].astype(BF)
        for j in range(3):
            mg_copies[g, j] = guarded(
                y > j, mg_send.at[g], mg_recv.at[g, j], mg_s.at[g, j], mg_r.at[g, j], below[j]
            )
        hs_send[g] = kgt[g, :, 0:HDR].T.astype(BF).reshape(8, 32, 128)
        for j in range(7):
            peer = (s + j + 1) % 8
            hs_copies[g, j] = go_out(
                hs_send.at[g, peer], hs_recv.at[g, j], hs_s.at[g, j], hs_r.at[g, j], seg_peer[j]
            )

    def close_a(g):
        rog[g] = jnp.zeros((128, 128), F32)
        for j in range(3):

            @pl.when(y + j + 1 < 4)
            def _():
                mg_copies[g, j].wait_recv()
                rog[g] += mg_recv[g, j].astype(F32)

        own = jnp.where(xl == 1, kgt[g, :, HDR : HDR + MEM], 0.0)
        pm_send[g] = (rog[g] + own).astype(BF)
        pm_copies[g] = go_out(pm_send.at[g], pm_recv.at[g], mg_s.at[g, 3], mg_r.at[g, 3], pair)
        total = hs_send[g, s].astype(F32)
        for j in range(7):
            hs_copies[g, j].wait_recv()
            total = total + hs_recv[g, j].astype(F32)
        hg[g] = total.astype(BF)
        hcopy = go_out(hg.at[g], hg_sib.at[g], sib_s.at[4 + g], sib_r.at[4 + g], sib)
        sib_copies[g] = [hcopy]

    def close_b(g):
        pm_copies[g].wait_recv()
        later = (rog[g] + pm_recv[g].astype(F32)).astype(BF)
        back = jnp.dot(later, rw[g], preferred_element_type=F32)
        vgt[0, g] = (kgt[g, :, HDR + MEM : NK] + back).astype(BF)
        sib_copies[g].append(
            go_out(vgt.at[0, g], vgt.at[1, g], sib_s.at[g], sib_r.at[g], sib)
        )

    sib_x = remote(
        xall.at[:, pl.ds(0, 256)], xall.at[:, pl.ds(256, 256)], x_sem.at[0], x_sem.at[1], sib
    )
    sib_hx = remote(
        xall.at[:, pl.ds(512, 32)], xall.at[:, pl.ds(544, 32)], x_sem.at[2], x_sem.at[3], sib
    )

    def x_ready():
        for rows, sem in ((pl.ds(0, 256), load_sem.at[8]), (pl.ds(512, 32), load_sem.at[9])):
            pltpu.make_async_copy(xall.at[:, rows], xall.at[:, rows], sem).wait()
        sib_x.wait_recv()
        sib_hx.wait_recv()

    def weigh(g):
        for copy in sib_copies[g]:
            copy.wait_recv()
        vgcat[:, 0:256] = vgt[0, g]
        vgcat[:, 256:512] = vgt[1, g]
        head = jnp.concatenate(
            [hg[g].astype(F32), hg_sib[g].astype(F32), jnp.zeros((64, 128), F32)], axis=0
        )
        vgcat[:, 512:640] = head.T.astype(BF)

        @pl.loop(0, 8)
        def _(k):
            for kh in range(2):
                grad = jnp.dot(vgcat[...], xall[kh * 8 + k], preferred_element_type=F32)
                grad = grad.astype(BF)
                for yy in range(4):
                    for xx in range(2):
                        i = (yy * 2 + xx) * 16
                        r1[g, yy, kh * 2 + xx, k] = grad[i : i + 16, 0:128]
                        r2[g, kh * 2 + xx, yy, k] = grad[i : i + 16, 128:256]

    first = {}
    second = {}
    last = {}
    spread = {}

    def rs_1(g):
        if g == G - 1:
            first[g] = (
                rs_direct(r1.at[g], da1, "y", 4 + 4 * g),
                rs_direct(r2.at[g], da2, "x", 5 + 4 * g),
            )
        else:
            first[g] = (
                rs_start(r1.at[g], ra1.at[g], "y", 4, 4 + 4 * g),
                rs_start(r2.at[g], ra2.at[g], "x", 4, 5 + 4 * g),
            )

    def rs_2(g):
        rs_forward(r1.at[g], ra1.at[g], "y", 4, 4 + 4 * g, first[g][0])
        rs_forward(r2.at[g], ra2.at[g], "x", 4, 5 + 4 * g, first[g][1])

    def rs_3(g):
        if g == G - 1:
            rs_sum(r1.at[g], da1, s1.at[g], "y", first[g][0])
        else:
            rs_end(r1.at[g], ra1.at[g], s1.at[g], "y", 4, first[g][0])
        one = rs_direct(s1.at[g], rb1.at[g], "x", 6 + 4 * g)
        if g == G - 1:
            rs_sum(r2.at[g], da2, s2.at[g], "x", first[g][1])
        else:
            rs_end(r2.at[g], ra2.at[g], s2.at[g], "x", 4, first[g][1])
        second[g] = (one, rs_direct(s2.at[g], rb2.at[g], "y", 7 + 4 * g))

    def rs_5(g):
        last[g] = []
        for part, (s_ref, rb, t_ref, zr, axis) in enumerate(
            ((s1, rb1, t1, zr1, "x"), (s2, rb2, t2, zr2, "y"))
        ):
            rs_sum(s_ref.at[g], rb.at[g], t_ref.at[g], axis, second[g][part])
            for j in (3, 2, 4, 1, 5, 0, 6):
                to = (z + j + 1) % 8
                st = 2 + 2 * g + part
                last[g].append(
                    go_out(
                        t_ref.at[g, to], zr.at[g, j], z_s.at[st, j], z_r.at[st, j], z_peer[j]
                    )
                )

    def rs_6(g):
        for copy in last[g]:
            copy.wait_recv()
        for t_ref, zr, cols in ((t1, zr1, slice(0, 128)), (t2, zr2, slice(128, 256))):
            total = t_ref[g, z].astype(F32)
            for j in range(7):
                total = total + zr[g, j].astype(F32)
            fall[g, s, :, cols] = total
        spread[g] = [
            go_out(fall.at[g, s], fall.at[g, s], f_s.at[g, j], f_r.at[g, j], seg_peer[j])
            for j in range(7)
        ]

    def rs_7(g):
        for copy in spread[g]:
            copy.wait_recv()
        dw_ref[:, g * 128 : g * 128 + 128] = fall[g].reshape(128, 256).T

    attend(0, 0)
    attend(0, 1)
    for copy in own_w:
        copy.wait()
    for copy in wz_copies:
        copy.wait_recv()
    near = ag_direct(wb1.at[y], "x", 0) + ag_direct(wb2.at[x], "y", 1)
    attend(1, 0)
    attend(1, 1)
    close_a(0)
    for copy in near:
        copy.wait_recv()
    wy1 = ag_start(wb1, "y", 4, 2)
    wx2 = ag_start(wb2, "x", 4, 3)
    attend(2, 0)
    close_b(0)
    attend(2, 1)
    close_a(1)
    x_ready()
    weigh(0)
    rs_1(0)
    attend(3, 0)
    close_b(1)
    weigh(1)
    rs_1(1)
    attend(3, 1)
    close_a(2)
    ag_forward(wb1, "y", 4, 2, wy1)
    ag_forward(wb2, "x", 4, 3, wx2)
    rs_2(0)
    close_b(2)
    weigh(2)
    rs_1(2)
    close_a(3)
    rs_3(0)
    rs_2(1)
    close_b(3)
    weigh(3)
    rs_1(3)

    ag_end(wy1)
    ag_end(wx2)
    for q in range(4):
        xs, ws = [], []
        for k in range(4 * q, 4 * q + 4):
            kh, kz = k // 8, k % 8
            xs.append(xall[k, 0:576])
            for yy in range(4):
                for xx in range(2):
                    ws.append(wb1[yy, kh * 2 + xx, kz])
                    ws.append(wb2[kh * 2 + xx, yy, kz])
        part = jnp.dot(
            jnp.concatenate(xs, axis=1), jnp.concatenate(ws, axis=0), preferred_element_type=F32
        )
        if q == 0:
            acc[...] = part
        else:
            acc[...] += part
    va = go_out(
        acc.at[pl.ds(256, 256)], vrecv.at[pl.ds(0, 256)], sib_s.at[8], sib_r.at[8], sib
    )
    vb = go_out(acc.at[pl.ds(544, 32)], vrecv.at[pl.ds(256, 32)], sib_s.at[9], sib_r.at[9], sib)
    rs_3(1)
    rs_2(2)
    rs_5(0)
    va.wait_recv()
    vb.wait_recv()
    hv_all[s] = (acc[512:544] + vrecv[256:288]).astype(BF)
    hv_copies = [
        go_out(hv_all.at[s], hv_all.at[s], seg_s.at[1, j], seg_r.at[1, j], seg_peer[j])
        for j in range(7)
    ]
    v_all[...] = (acc[0:256] + vrecv[0:256]).astype(BF)
    for g in range(G):
        cg = slice(g * 128, g * 128 + 128)
        ro_send[:, cg] = jnp.dot(rw[g], v_all[:, cg], preferred_element_type=F32).astype(BF)
    ro_copies = [
        guarded(
            y + j + 1 < 4, ro_send, ro_recv.at[j], seg_s.at[2, j], seg_r.at[2, j], above[j]
        )
        for j in range(3)
    ]
    rs_3(2)
    rs_5(1)
    rs_6(0)

    memory[...] = jnp.zeros((MEM, 512), F32)
    for j in range(3):

        @pl.when(y > j)
        def _():
            ro_copies[j].wait_recv()
            memory[...] += ro_recv[j].astype(F32)

    po_send[...] = (memory[...] + jnp.where(xl == 0, ro_send[...].astype(F32), 0.0)).astype(BF)
    po_copy = go_out(po_send, po_recv, seg_s.at[2, 3], seg_r.at[2, 3], pair)
    rs_3(3)
    rs_5(2)
    rs_6(1)
    rs_7(0)
    for copy in hv_copies:
        copy.wait_recv()
    po_copy.wait_recv()
    for g in range(G):
        cg = slice(g * 128, g * 128 + 128)
        for t in range(8):
            vcat[g, t * 32 : t * 32 + 32] = hv_all[t, :, cg]
        total = minit[0, :, cg] + memory[:, cg] + po_recv[:, cg].astype(F32)
        vcat[g, 256:384] = total.astype(BF)
        vcat[g, 384:640] = v_all[:, cg]

    out_copies = []

    def finish(g):
        @pl.loop(0, T // 2)
        def _(t):
            for u in range(2):
                h = g * T + 2 * t + u
                cols = pl.ds(pl.multiple_of(h * 128, 128), 128)
                part = jnp.dot(wts[h], vcat[g], preferred_element_type=F32)
                out_v[:, cols] = part.astype(BF)

        cols = pl.ds(g * 1024, 1024)
        copy = pltpu.make_async_copy(
            out_v.at[:, cols], out_hbm.at[0, 0, :, cols], load_sem.at[12 + g]
        )
        copy.start()
        out_copies.append(copy)

    finish(0)
    rs_5(3)
    rs_6(2)
    rs_7(1)
    finish(1)
    rs_6(3)
    finish(2)
    rs_7(2)
    finish(3)
    rs_7(3)

    for copy in out_copies:
        copy.wait()
    sib_x.wait_send()
    sib_hx.wait_send()
    for condition, copy in sends:
        if condition is None:
            copy.wait_send()
        else:
            pl.when(condition)(copy.wait_send)


def per_device(*args):
    vmem = pl.BlockSpec(memory_space=pltpu.VMEM)
    hbm = pl.BlockSpec(memory_space=pl.ANY)
    smem = pl.BlockSpec(memory_space=pltpu.SMEM)
    V = pltpu.VMEM
    dma = pltpu.SemaphoreType.DMA
    return pl.pallas_call(
        kernel,
        out_shape=(
            jax.ShapeDtypeStruct((1, 1, SEG, 4096), BF),
            jax.ShapeDtypeStruct((256, 512), F32),
        ),
        in_specs=[hbm, hbm, hbm, vmem, vmem, vmem, vmem, vmem, smem, hbm, hbm],
        out_specs=(hbm, vmem),
        scratch_shapes=[
            V((SEG, 4096), BF),
            V((SEG, 4096), BF),
            V((SEG, 4096), BF),
            V((32, SEG, NK), BF),
            V((G, NK, HD), BF),
            V((8, 32, 512), BF),
            V((SEG, NK), F32),
            V((G, MEM, SEG), BF),
            V((G, HD, NK), F32),
            V((16, 640, 256), BF),
            V((4, 4, 8, 16, 512), BF),
            V((4, 4, 8, 16, 512), BF),
            V((G, HD, MEM), BF),
            V((G, 3, HD, MEM), BF),
            V((G, HD, MEM), BF),
            V((G, HD, MEM), BF),
            V((G, HD, MEM), F32),
            V((G, 8, 32, HD), BF),
            V((G, 7, 32, HD), BF),
            V((G, 32, HD), BF),
            V((G, 32, HD), BF),
            V((2, G, HD, SEG), BF),
            V((HD, 640), BF),
            V((G, 4, 4, 8, 16, 128), BF),
            V((G, 4, 4, 8, 16, 128), BF),
            V((G - 1, 6, 2, 8, 16, 128), BF),
            V((G - 1, 6, 2, 8, 16, 128), BF),
            V((3, 4, 8, 16, 128), BF),
            V((3, 4, 8, 16, 128), BF),
            V((G, 4, 8, 16, 128), BF),
            V((G, 4, 8, 16, 128), BF),
            V((G, 3, 8, 16, 128), BF),
            V((G, 3, 8, 16, 128), BF),
            V((G, 8, 16, 128), BF),
            V((G, 8, 16, 128), BF),
            V((G, 7, 16, 128), BF),
            V((G, 7, 16, 128), BF),
            V((G, 8, 16, 256), F32),
            V((576, 512), F32),
            V((288, 512), F32),
            V((SEG, 512), BF),
            V((8, 32, 512), BF),
            V((MEM, 512), BF),
            V((3, MEM, 512), BF),
            V((MEM, 512), BF),
            V((MEM, 512), BF),
            V((MEM, 512), F32),
            V((G, NK, HD), BF),
            dma((16,)),
            dma((4,)),
            dma((3, 7)),
            dma((3, 7)),
            dma((G, 7)),
            dma((G, 7)),
            dma((G, 4)),
            dma((G, 4)),
            dma((G, 7)),
            dma((G, 7)),
            dma((10,)),
            dma((10,)),
            dma((2 + 2 * G, 7)),
            dma((2 + 2 * G, 7)),
            dma((4 + 4 * G, 6)),
            dma((4 + 4 * G, 6)),
        ],
        compiler_params=pltpu.CompilerParams(
            collective_id=0, has_side_effects=True, vmem_limit_bytes=56 * 1024 * 1024
        ),
    )(*args)


def solution(mesh):
    placed = (
        P("dp", "seg", None, None),
        P("dp", "seg", None),
        P("dp", "seg", None, None),
        P("dp", "seg", None, None),
        P("dp", "seg", None, None),
        P("dp", "seg", None, None),
        P("dp", "seg", None),
        P("dp", None, None),
        P("dp", "seg", None, None),
        P("dp", "seg", None, None),
        P("dp", None),
    )
    return jax.shard_map(
        per_device,
        mesh=mesh,
        in_specs=placed,
        out_specs=(P("dp", "seg", None, None), P("dp", None)),
        check_vma=False,
    )
```

```python
import functools

import jax
import jax.numpy as jnp
from jax import lax
from jax.experimental import pallas as pl
from jax.experimental.pallas import tpu as pltpu
from jax.sharding import PartitionSpec as P

MESH = pl.DeviceIdType.MESH
BF = jnp.bfloat16
F32 = jnp.float32
NEG = -1e30
HD = 128
SEG = 256
MEM = 128
HDR = 256
G = 4
T = 8
HEADS = 4
NK = HDR + MEM + SEG
LOG2E = 1.4426950408889634
SCALE2 = HD ** (-0.5) * LOG2E


def device(x, y, z, c):
    return {"seg": y * 2 + x % 2, "dp": (x // 2) * 16 + z * 2 + c}


def kernel(
    seg_x,
    hdr_x,
    q_hbm,
    keys_hbm,
    memq_hbm,
    memk_hbm,
    hkeys_hbm,
    minit_hbm,
    mask,
    go_hbm,
    w_hbm,
    out_ref,
    dw_ref,
    keys,
    memq,
    memk,
    hkeys,
    minit,
    q_v,
    go_v,
    wts,
    kall,
    hk_all,
    bias,
    rw,
    kgt,
    xall,
    wa,
    wb2,
    mg_send,
    mg_recv,
    pm_send,
    pm_recv,
    rog,
    hs_send,
    hs_recv,
    hg,
    hg_sib,
    vgt,
    vgcat,
    r1,
    r2,
    ra1,
    ra2,
    da1,
    da2,
    s1,
    s2,
    rb1,
    rb2,
    t1,
    t2,
    zr1,
    zr2,
    fall,
    acc,
    vrecv,
    v_all,
    hv_all,
    ro_send,
    ro_recv,
    po_send,
    po_recv,
    memory,
    vcat,
    load_sem,
    x_sem,
    seg_s,
    seg_r,
    f_s,
    f_r,
    mg_s,
    mg_r,
    hs_s,
    hs_r,
    sib_s,
    sib_r,
    z_s,
    z_r,
    ring_s,
    ring_r,
):
    s = lax.axis_index("seg")
    p = lax.axis_index("dp")
    y, xl = s // 2, s % 2
    xh, z, c = p // 16, (p // 2) % 8, p % 2
    x = xh * 2 + xl
    k_own = xh * 8 + z
    sib = {"seg": s, "dp": xh * 16 + z * 2 + (1 - c)}
    seg_peer = [{"seg": (s + j) % 8, "dp": p} for j in range(1, 8)]
    pair = {"seg": y * 2 + (1 - xl), "dp": p}
    below = [{"seg": ((y + 4 - j) % 4) * 2 + xl, "dp": p} for j in (1, 2, 3)]
    above = [{"seg": ((y + j) % 4) * 2 + xl, "dp": p} for j in (1, 2, 3)]
    z_peer = [device(x, y, (z + j) % 8, c) for j in range(1, 8)]
    rings = {
        "x": (x, device((x + 1) % 4, y, z, c), device((x + 3) % 4, y, z, c)),
        "y": (y, device(x, (y + 1) % 4, z, c), device(x, (y + 3) % 4, z, c)),
    }
    sends = []

    def remote(src, dst, ssem, rsem, dev):
        return pltpu.make_async_remote_copy(
            src_ref=src,
            dst_ref=dst,
            send_sem=ssem,
            recv_sem=rsem,
            device_id=dev,
            device_id_type=MESH,
        )

    def go_out(src, dst, ssem, rsem, dev):
        copy = remote(src, dst, ssem, rsem, dev)
        copy.start()
        sends.append((None, copy))
        return copy

    small = [
        pltpu.make_async_copy(src, dst, load_sem.at[12 + i])
        for i, (src, dst) in enumerate(
            (
                (hkeys_hbm, hkeys),
                (keys_hbm, keys),
                (memq_hbm, memq),
                (memk_hbm, memk),
                (minit_hbm, minit),
            )
        )
    ]
    for copy in small:
        copy.start()
    loads = []
    for g in range(G):
        cols = pl.ds(g * 1024, 1024)
        a = pltpu.make_async_copy(q_hbm.at[0, 0, :, cols], q_v.at[:, cols], load_sem.at[2 * g])
        b = pltpu.make_async_copy(go_hbm.at[0, 0, :, cols], go_v.at[:, cols], load_sem.at[2 * g + 1])
        a.start()
        b.start()
        loads.append((a, b))

    @pl.loop(0, 16)
    def _(k):
        cols = pl.ds(pl.multiple_of((2 * k + c) * 256, 256), 256)
        pltpu.make_async_copy(
            seg_x.at[0, 0, :, cols], xall.at[k, pl.ds(0, 256)], load_sem.at[8]
        ).start()
        pltpu.make_async_copy(
            hdr_x.at[0, :, cols], xall.at[k, pl.ds(512, 32)], load_sem.at[9]
        ).start()

    top_rows = w_hbm.at[pl.ds(0, 128)]
    piece = w_hbm.at[pl.ds(pl.multiple_of(128 + s * 16, 16), 16)]
    own_w = [
        pltpu.make_async_copy(top_rows, wa.at[xh, z], load_sem.at[10]),
        pltpu.make_async_copy(piece, wb2.at[x, y, z], load_sem.at[11]),
    ]
    for copy in own_w:
        copy.start()

    barrier = pltpu.get_barrier_semaphore()
    across = [device((x + j) % 4, y, z, c) for j in (1, 2, 3)]
    greeted = [sib] + across + seg_peer + z_peer
    for dev in greeted:
        pl.semaphore_signal(barrier, inc=1, device_id=dev, device_id_type=MESH)
    pl.semaphore_wait(barrier, len(greeted))

    for copy in small:
        copy.wait()

    hk_copies = [
        go_out(hkeys.at[0], hk_all.at[s], seg_s.at[0, j], seg_r.at[0, j], seg_peer[j])
        for j in range(7)
    ]
    far_first = (3, 2, 4, 1, 5, 0, 6)
    wz_copies = [
        go_out(piece, wb2.at[x, y, z], z_s.at[1, j], z_r.at[1, j], z_peer[j]) for j in far_first
    ]
    beside = go_out(
        top_rows, wa.at[xh, z], ring_s.at[0, 0], ring_r.at[0, 0], device(3 - x, y, z, c)
    )
    wa_copies = [
        go_out(top_rows, wa.at[xh, z], z_s.at[0, j], z_r.at[0, j], z_peer[j]) for j in far_first
    ]

    @pl.loop(0, 16)
    def _(k):
        cols = pl.ds(pl.multiple_of((2 * k + 1 - c) * 256, 256), 256)
        remote(
            seg_x.at[0, 0, :, cols], xall.at[k, pl.ds(256, 256)], x_sem.at[0], x_sem.at[1], sib
        ).start()
        remote(
            hdr_x.at[0, :, cols], xall.at[k, pl.ds(544, 32)], x_sem.at[2], x_sem.at[3], sib
        ).start()

    hk_all[s] = hkeys[0]
    for k in range(16):
        xall[k, 576:640] = jnp.zeros((64, 256), BF)

    rows_i = lax.broadcasted_iota(jnp.int32, (128, 128), 0)
    cols_i = lax.broadcasted_iota(jnp.int32, (128, 128), 1)
    causal = jnp.where(cols_i <= rows_i, 0.0, NEG).astype(F32)
    for qb in range(2):
        for kb in range(5):
            level = jnp.where(mask[0, 0, qb, kb] > 0, 0.0, NEG).astype(F32)
            block = jnp.full((128, 128), level, F32)
            if kb == 3 + qb:
                block = jnp.minimum(block, causal)
            bias[qb * 128 : qb * 128 + 128, kb * 128 : kb * 128 + 128] = block

    def softmax2(scores):
        top = jnp.max(scores, axis=-1, keepdims=True)
        e = jnp.exp2(scores - top)
        return e * (1.0 / jnp.sum(e, axis=-1, keepdims=True))

    nt = (((1,), (1,)), ((), ()))
    tn = (((0,), (0,)), ((), ()))
    for g in range(G):
        cg = slice(g * 128, g * 128 + 128)
        kall[g, 256:384] = memk[0, 0, :, cg]
        kall[g, 384:640] = keys[0, 0, :, cg]
        sc = lax.dot_general(memq[0, 0, :, cg], keys[0, 0, :, cg], nt, preferred_element_type=F32)
        rw[g] = softmax2(sc * SCALE2).astype(BF)

    for copy in hk_copies:
        copy.wait_recv()
    for g in range(G):
        for t in range(8):
            kall[g, t * 32 : t * 32 + 32] = hk_all[t, :, g * 128 : g * 128 + 128]

    def ag_start(buf, axis, n, st):
        r, right, left = rings[axis]
        lo, hi = pl.ds(0, n // 2), pl.ds(n // 2, n // 2)
        S, R = ring_s.at[st], ring_r.at[st]
        cp = {}
        cp["Llo"] = go_out(buf.at[r, lo], buf.at[r, lo], S.at[0], R.at[0], right)
        cp["Rhi"] = go_out(buf.at[r, hi], buf.at[r, hi], S.at[3], R.at[3], left)
        cp["Lhi"] = go_out(buf.at[r, hi], buf.at[r, hi], S.at[1], R.at[1], right)
        cp["Rlo"] = go_out(buf.at[r, lo], buf.at[r, lo], S.at[2], R.at[2], left)
        return cp

    def ag_forward(buf, axis, n, st, cp):
        r, right, left = rings[axis]
        lo, hi = pl.ds(0, n // 2), pl.ds(n // 2, n // 2)
        S, R = ring_s.at[st], ring_r.at[st]
        before, after = (r + 3) % 4, (r + 1) % 4
        cp["Llo"].wait_recv()
        cp["FL"] = go_out(buf.at[before, lo], buf.at[before, lo], S.at[4], R.at[4], right)
        cp["Rhi"].wait_recv()
        cp["FR"] = go_out(buf.at[after, hi], buf.at[after, hi], S.at[5], R.at[5], left)

    def ag_end(cp):
        for name in ("Lhi", "Rlo", "FL", "FR"):
            cp[name].wait_recv()

    around = {
        "x": (x, [device((x + j) % 4, y, z, c) for j in (1, 2, 3)]),
        "y": (y, [device(x, (y + j) % 4, z, c) for j in (1, 2, 3)]),
    }

    def ag_direct(buf, axis, st):
        r, to = around[axis]
        S, R = ring_s.at[st], ring_r.at[st]
        return [go_out(buf.at[r], buf.at[r], S.at[j], R.at[j], to[j]) for j in (1, 0, 2)]

    def rs_direct(buf, land, axis, st):
        r, to = around[axis]
        S, R = ring_s.at[st], ring_r.at[st]
        return [
            go_out(buf.at[(r + j + 1) % 4], land.at[j], S.at[j], R.at[j], to[j])
            for j in (1, 0, 2)
        ]

    def rs_sum(buf, land, out, axis, copies):
        for copy in copies:
            copy.wait_recv()
        total = buf[around[axis][0]].astype(F32)
        for j in range(3):
            total = total + land[j].astype(F32)
        out[...] = total.astype(BF)

    def rs_start(buf, land, axis, n, st):
        r, right, left = rings[axis]
        lo, hi = pl.ds(0, n // 2), pl.ds(n // 2, n // 2)
        S, R = ring_s.at[st], ring_r.at[st]
        far, after, before = (r + 2) % 4, (r + 1) % 4, (r + 3) % 4
        cp = {}
        cp["PL"] = go_out(buf.at[far, lo], land.at[0], S.at[0], R.at[0], right)
        cp["PR"] = go_out(buf.at[far, hi], land.at[1], S.at[1], R.at[1], left)
        cp["Lhi"] = go_out(buf.at[after, hi], land.at[3], S.at[3], R.at[3], right)
        cp["Rlo"] = go_out(buf.at[before, lo], land.at[4], S.at[4], R.at[4], left)
        return cp

    def rs_forward(buf, land, axis, n, st, cp):
        r, right, left = rings[axis]
        half = n // 2
        lo, hi = pl.ds(0, half), pl.ds(half, half)
        S, R = ring_s.at[st], ring_r.at[st]
        after, before = (r + 1) % 4, (r + 3) % 4
        cp["PL"].wait_recv()
        buf[after, lo] = (buf[after, lo].astype(F32) + land[0].astype(F32)).astype(BF)
        cp["Llo"] = go_out(buf.at[after, lo], land.at[2], S.at[2], R.at[2], right)
        cp["PR"].wait_recv()
        buf[before, hi] = (buf[before, hi].astype(F32) + land[1].astype(F32)).astype(BF)
        cp["Rhi"] = go_out(buf.at[before, hi], land.at[5], S.at[5], R.at[5], left)

    def rs_end(buf, land, out, axis, n, cp):
        r = rings[axis][0]
        half = n // 2
        for name in ("Lhi", "Rlo", "Llo", "Rhi"):
            cp[name].wait_recv()
        for part in range(2):
            here = pl.ds(half * part, half)
            a = buf[r, here].astype(F32) + land[2 + part].astype(F32)
            out[here] = (a + land[4 + part].astype(F32)).astype(BF)

    def guarded(condition, src, dst, ssem, rsem, dev):
        copy = remote(src, dst, ssem, rsem, dev)
        pl.when(condition)(copy.start)
        sends.append((condition, copy))
        return copy

    mg_copies = {}
    pm_copies = {}
    hs_copies = {}
    sib_copies = {}

    def attend(g, part):
        if part == 0:
            loads[g][0].wait()
            loads[g][1].wait()
            kgt[g] = jnp.zeros((128, NK), F32)

        @pl.loop(0, T // 2 // HEADS)
        def _(t):
            for u in range(HEADS):
                h = g * T + part * (T // 2) + t * HEADS + u
                cols = pl.ds(pl.multiple_of(h * 128, 128), 128)
                for qb in range(2):
                    nk = 512 + 128 * qb
                    rows = slice(qb * 128, qb * 128 + 128)
                    sc = lax.dot_general(
                        q_v[rows, cols], kall[g, 0:nk], nt, preferred_element_type=F32
                    )
                    wt = softmax2(sc * SCALE2 + bias[rows, 0:nk]).astype(BF)
                    wts[h, rows, 0:nk] = wt
                    if qb == 0:
                        wts[h, rows, 512:640] = jnp.zeros((128, 128), BF)
            for u in range(HEADS):
                h = g * T + part * (T // 2) + t * HEADS + u
                cols = pl.ds(pl.multiple_of(h * 128, 128), 128)
                kgt[g] += lax.dot_general(go_v[:, cols], wts[h], tn, preferred_element_type=F32)

        if part == 0:
            return
        mg_send[g] = kgt[g, :, HDR : HDR + MEM].astype(BF)
        for j in range(3):
            mg_copies[g, j] = guarded(
                y > j, mg_send.at[g], mg_recv.at[g, j], mg_s.at[g, j], mg_r.at[g, j], below[j]
            )
        hs_send[g] = kgt[g, :, 0:HDR].T.astype(BF).reshape(8, 32, 128)
        for j in range(7):
            peer = (s + j + 1) % 8
            hs_copies[g, j] = go_out(
                hs_send.at[g, peer], hs_recv.at[g, j], hs_s.at[g, j], hs_r.at[g, j], seg_peer[j]
            )

    def close_a(g):
        rog[g] = jnp.zeros((128, 128), F32)
        for j in range(3):

            @pl.when(y + j + 1 < 4)
            def _():
                mg_copies[g, j].wait_recv()
                rog[g] += mg_recv[g, j].astype(F32)

        own = jnp.where(xl == 1, kgt[g, :, HDR : HDR + MEM], 0.0)
        pm_send[g] = (rog[g] + own).astype(BF)
        pm_copies[g] = go_out(pm_send.at[g], pm_recv.at[g], mg_s.at[g, 3], mg_r.at[g, 3], pair)
        total = hs_send[g, s].astype(F32)
        for j in range(7):
            hs_copies[g, j].wait_recv()
            total = total + hs_recv[g, j].astype(F32)
        hg[g] = total.astype(BF)
        hcopy = go_out(hg.at[g], hg_sib.at[g], sib_s.at[4 + g], sib_r.at[4 + g], sib)
        sib_copies[g] = [hcopy]

    def close_b(g):
        pm_copies[g].wait_recv()
        later = (rog[g] + pm_recv[g].astype(F32)).astype(BF)
        back = jnp.dot(later, rw[g], preferred_element_type=F32)
        vgt[0, g] = (kgt[g, :, HDR + MEM : NK] + back).astype(BF)
        sib_copies[g].append(
            go_out(vgt.at[0, g], vgt.at[1, g], sib_s.at[g], sib_r.at[g], sib)
        )

    sib_x = remote(
        xall.at[:, pl.ds(0, 256)], xall.at[:, pl.ds(256, 256)], x_sem.at[0], x_sem.at[1], sib
    )
    sib_hx = remote(
        xall.at[:, pl.ds(512, 32)], xall.at[:, pl.ds(544, 32)], x_sem.at[2], x_sem.at[3], sib
    )

    def x_ready():
        for rows, sem in ((pl.ds(0, 256), load_sem.at[8]), (pl.ds(512, 32), load_sem.at[9])):
            pltpu.make_async_copy(xall.at[:, rows], xall.at[:, rows], sem).wait()
        sib_x.wait_recv()
        sib_hx.wait_recv()

    def weigh(g):
        for copy in sib_copies[g]:
            copy.wait_recv()
        vgcat[:, 0:256] = vgt[0, g]
        vgcat[:, 256:512] = vgt[1, g]
        head = jnp.concatenate(
            [hg[g].astype(F32), hg_sib[g].astype(F32), jnp.zeros((64, 128), F32)], axis=0
        )
        vgcat[:, 512:640] = head.T.astype(BF)

        @pl.loop(0, 8)
        def _(k):
            for kh in range(2):
                grad = jnp.dot(vgcat[...], xall[kh * 8 + k], preferred_element_type=F32)
                grad = grad.astype(BF)
                for yy in range(4):
                    for xx in range(2):
                        i = (yy * 2 + xx) * 16
                        r1[g, yy, kh * 2 + xx, k] = grad[i : i + 16, 0:128]
                        r2[g, kh * 2 + xx, yy, k] = grad[i : i + 16, 128:256]

    first = {}
    second = {}
    last = {}
    spread = {}

    def rs_1(g):
        if g == G - 1:
            first[g] = (
                rs_direct(r1.at[g], da1, "y", 4 + 4 * g),
                rs_direct(r2.at[g], da2, "x", 5 + 4 * g),
            )
        else:
            first[g] = (
                rs_start(r1.at[g], ra1.at[g], "y", 4, 4 + 4 * g),
                rs_start(r2.at[g], ra2.at[g], "x", 4, 5 + 4 * g),
            )

    def rs_2(g):
        rs_forward(r1.at[g], ra1.at[g], "y", 4, 4 + 4 * g, first[g][0])
        rs_forward(r2.at[g], ra2.at[g], "x", 4, 5 + 4 * g, first[g][1])

    def rs_3(g):
        if g == G - 1:
            rs_sum(r1.at[g], da1, s1.at[g], "y", first[g][0])
        else:
            rs_end(r1.at[g], ra1.at[g], s1.at[g], "y", 4, first[g][0])
        one = rs_direct(s1.at[g], rb1.at[g], "x", 6 + 4 * g)
        if g == G - 1:
            rs_sum(r2.at[g], da2, s2.at[g], "x", first[g][1])
        else:
            rs_end(r2.at[g], ra2.at[g], s2.at[g], "x", 4, first[g][1])
        second[g] = (one, rs_direct(s2.at[g], rb2.at[g], "y", 7 + 4 * g))

    def rs_5(g):
        last[g] = []
        for part, (s_ref, rb, t_ref, zr, axis) in enumerate(
            ((s1, rb1, t1, zr1, "x"), (s2, rb2, t2, zr2, "y"))
        ):
            rs_sum(s_ref.at[g], rb.at[g], t_ref.at[g], axis, second[g][part])
            for j in (3, 2, 4, 1, 5, 0, 6):
                to = (z + j + 1) % 8
                st = 2 + 2 * g + part
                last[g].append(
                    go_out(
                        t_ref.at[g, to], zr.at[g, j], z_s.at[st, j], z_r.at[st, j], z_peer[j]
                    )
                )

    def rs_6(g):
        for copy in last[g]:
            copy.wait_recv()
        for t_ref, zr, cols in ((t1, zr1, slice(0, 128)), (t2, zr2, slice(128, 256))):
            total = t_ref[g, z].astype(F32)
            for j in range(7):
                total = total + zr[g, j].astype(F32)
            fall[g, s, :, cols] = total
        spread[g] = [
            go_out(fall.at[g, s], fall.at[g, s], f_s.at[g, j], f_r.at[g, j], seg_peer[j])
            for j in range(7)
        ]

    def rs_7(g):
        for copy in spread[g]:
            copy.wait_recv()
        dw_ref[:, g * 128 : g * 128 + 128] = fall[g].reshape(128, 256).T

    attend(0, 0)
    attend(0, 1)
    for copy in own_w:
        copy.wait()
    for copy in wz_copies:
        copy.wait_recv()
    near = ag_direct(wb2.at[x], "y", 1)
    beside.wait_recv()
    other = wa.at[1 - xh, z]
    st = 2 + 2 * G
    for j in far_first:
        wa_copies.append(go_out(other, other, z_s.at[st, j], z_r.at[st, j], z_peer[j]))
    attend(1, 0)
    attend(1, 1)
    close_a(0)
    for copy in near:
        copy.wait_recv()
    wx2 = ag_start(wb2, "x", 4, 3)
    attend(2, 0)
    close_b(0)
    attend(2, 1)
    close_a(1)
    x_ready()
    weigh(0)
    rs_1(0)
    attend(3, 0)
    close_b(1)
    weigh(1)
    rs_1(1)
    attend(3, 1)
    close_a(2)
    ag_forward(wb2, "x", 4, 3, wx2)
    rs_2(0)
    close_b(2)
    weigh(2)
    rs_1(2)
    close_a(3)
    rs_3(0)
    rs_2(1)
    close_b(3)
    weigh(3)
    rs_1(3)

    ag_end(wx2)
    for copy in wa_copies:
        copy.wait_recv()
    for q in range(4):
        xs, ws = [], []
        for k in range(4 * q, 4 * q + 4):
            kh, kz = k // 8, k % 8
            xs.append(xall[k, 0:576])
            ws.append(wa[kh, kz])
            for yy in range(4):
                for xx in range(2):
                    ws.append(wb2[kh * 2 + xx, yy, kz])
        part = jnp.dot(
            jnp.concatenate(xs, axis=1), jnp.concatenate(ws, axis=0), preferred_element_type=F32
        )
        if q == 0:
            acc[...] = part
        else:
            acc[...] += part
    va = go_out(
        acc.at[pl.ds(256, 256)], vrecv.at[pl.ds(0, 256)], sib_s.at[8], sib_r.at[8], sib
    )
    vb = go_out(acc.at[pl.ds(544, 32)], vrecv.at[pl.ds(256, 32)], sib_s.at[9], sib_r.at[9], sib)
    rs_3(1)
    rs_2(2)
    rs_5(0)
    va.wait_recv()
    vb.wait_recv()
    hv_all[s] = (acc[512:544] + vrecv[256:288]).astype(BF)
    hv_copies = [
        go_out(hv_all.at[s], hv_all.at[s], seg_s.at[1, j], seg_r.at[1, j], seg_peer[j])
        for j in range(7)
    ]
    v_all[...] = (acc[0:256] + vrecv[0:256]).astype(BF)
    for g in range(G):
        cg = slice(g * 128, g * 128 + 128)
        ro_send[:, cg] = jnp.dot(rw[g], v_all[:, cg], preferred_element_type=F32).astype(BF)
    ro_copies = [
        guarded(
            y + j + 1 < 4, ro_send, ro_recv.at[j], seg_s.at[2, j], seg_r.at[2, j], above[j]
        )
        for j in range(3)
    ]
    rs_3(2)
    rs_5(1)
    rs_6(0)

    memory[...] = jnp.zeros((MEM, 512), F32)
    for j in range(3):

        @pl.when(y > j)
        def _():
            ro_copies[j].wait_recv()
            memory[...] += ro_recv[j].astype(F32)

    po_send[...] = (memory[...] + jnp.where(xl == 0, ro_send[...].astype(F32), 0.0)).astype(BF)
    po_copy = go_out(po_send, po_recv, seg_s.at[2, 3], seg_r.at[2, 3], pair)
    rs_3(3)
    rs_5(2)
    rs_6(1)
    rs_7(0)
    for copy in hv_copies:
        copy.wait_recv()
    po_copy.wait_recv()
    for g in range(G):
        cg = slice(g * 128, g * 128 + 128)
        for t in range(8):
            vcat[g, t * 32 : t * 32 + 32] = hv_all[t, :, cg]
        total = minit[0, :, cg] + memory[:, cg] + po_recv[:, cg].astype(F32)
        vcat[g, 256:384] = total.astype(BF)
        vcat[g, 384:640] = v_all[:, cg]

    def finish(g):
        @pl.loop(0, T // 2)
        def _(t):
            for u in range(2):
                h = g * T + 2 * t + u
                cols = pl.ds(pl.multiple_of(h * 128, 128), 128)
                part = jnp.dot(wts[h], vcat[g], preferred_element_type=F32)
                out_ref[0, 0, :, cols] = part.astype(BF)

    finish(0)
    rs_5(3)
    rs_6(2)
    rs_7(1)
    finish(1)
    rs_6(3)
    finish(2)
    rs_7(2)
    finish(3)
    rs_7(3)

    sib_x.wait_send()
    sib_hx.wait_send()
    for condition, copy in sends:
        if condition is None:
            copy.wait_send()
        else:
            pl.when(condition)(copy.wait_send)


def per_device(*args):
    vmem = pl.BlockSpec(memory_space=pltpu.VMEM)
    hbm = pl.BlockSpec(memory_space=pl.ANY)
    smem = pl.BlockSpec(memory_space=pltpu.SMEM)
    V = pltpu.VMEM
    dma = pltpu.SemaphoreType.DMA
    return pl.pallas_call(
        kernel,
        out_shape=(
            pltpu.VMEM((1, 1, SEG, 4096), BF),
            pltpu.VMEM((256, 512), F32),
        ),
        in_specs=[hbm] * 8 + [smem, hbm, hbm],
        out_specs=(vmem, vmem),
        scratch_shapes=[
            V((1, 1, SEG, 512), BF),
            V((1, 1, MEM, 512), BF),
            V((1, 1, MEM, 512), BF),
            V((1, 32, 512), BF),
            V((1, MEM, 512), F32),
            V((SEG, 4096), BF),
            V((SEG, 4096), BF),
            V((32, SEG, NK), BF),
            V((G, NK, HD), BF),
            V((8, 32, 512), BF),
            V((SEG, NK), F32),
            V((G, MEM, SEG), BF),
            V((G, HD, NK), F32),
            V((16, 640, 256), BF),
            V((2, 8, 128, 512), BF),
            V((4, 4, 8, 16, 512), BF),
            V((G, HD, MEM), BF),
            V((G, 3, HD, MEM), BF),
            V((G, HD, MEM), BF),
            V((G, HD, MEM), BF),
            V((G, HD, MEM), F32),
            V((G, 8, 32, HD), BF),
            V((G, 7, 32, HD), BF),
            V((G, 32, HD), BF),
            V((G, 32, HD), BF),
            V((2, G, HD, SEG), BF),
            V((HD, 640), BF),
            V((G, 4, 4, 8, 16, 128), BF),
            V((G, 4, 4, 8, 16, 128), BF),
            V((G - 1, 6, 2, 8, 16, 128), BF),
            V((G - 1, 6, 2, 8, 16, 128), BF),
            V((3, 4, 8, 16, 128), BF),
            V((3, 4, 8, 16, 128), BF),
            V((G, 4, 8, 16, 128), BF),
            V((G, 4, 8, 16, 128), BF),
            V((G, 3, 8, 16, 128), BF),
            V((G, 3, 8, 16, 128), BF),
            V((G, 8, 16, 128), BF),
            V((G, 8, 16, 128), BF),
            V((G, 7, 16, 128), BF),
            V((G, 7, 16, 128), BF),
            V((G, 8, 16, 256), F32),
            V((576, 512), F32),
            V((288, 512), F32),
            V((SEG, 512), BF),
            V((8, 32, 512), BF),
            V((MEM, 512), BF),
            V((3, MEM, 512), BF),
            V((MEM, 512), BF),
            V((MEM, 512), BF),
            V((MEM, 512), F32),
            V((G, NK, HD), BF),
            dma((17,)),
            dma((4,)),
            dma((3, 7)),
            dma((3, 7)),
            dma((G, 7)),
            dma((G, 7)),
            dma((G, 4)),
            dma((G, 4)),
            dma((G, 7)),
            dma((G, 7)),
            dma((10,)),
            dma((10,)),
            dma((3 + 2 * G, 7)),
            dma((3 + 2 * G, 7)),
            dma((4 + 4 * G, 6)),
            dma((4 + 4 * G, 6)),
        ],
        compiler_params=pltpu.CompilerParams(
            collective_id=0, has_side_effects=True, vmem_limit_bytes=56 * 1024 * 1024
        ),
    )(*args)


def solution(mesh):
    placed = (
        P("dp", "seg", None, None),
        P("dp", "seg", None),
        P("dp", "seg", None, None),
        P("dp", "seg", None, None),
        P("dp", "seg", None, None),
        P("dp", "seg", None, None),
        P("dp", "seg", None),
        P("dp", None, None),
        P("dp", "seg", None, None),
        P("dp", "seg", None, None),
        P("dp", None),
    )
    return jax.shard_map(
        per_device,
        mesh=mesh,
        in_specs=placed,
        out_specs=(P("dp", "seg", None, None), P("dp", None)),
        check_vma=False,
    )
```
